32 devices in a mesh: level: 2 (over y), space: 16 (over z, x, core).
Axes of the slice: x: 2, y: 2, z: 4, core: 2. Of those that a mesh axis runs over, the one named last changes fastest.
Arguments:
- start: float32 [128, 64, 128], P('space'), may hold values from -6 to 6
- source: float32 [128, 64, 128], P('space'), may hold values from -6 to 6
- past_rates: float32 [2, 10, 128, 64, 128], P('level', None, 'space'), may hold values from -6 to 6
- block_ids: int32 [2048], P('space'), may hold values from 0 to 8191, as said below
- block_bits: int32 [2048, 5], P('space'), may hold values from 0 to 1073741823
- block_drag: float32 [2048], P('space'), may hold values from 0.5 to 4
Outputs:
- mean_rates: float32 [2, 128, 64, 128], P('level', 'space')
- defects: float32 [2, 128, 64, 128], P('level', 'space')
The draws below stay inside these ranges and needn't reach their ends.
Inputs may be any that keep to these rules, and one draw needn't show every extreme that they name: `block_ids`: entries s * 128 to (s + 1) * 128 - 1 name 128 distinct blocks z * 64 + x with z from s * 8 to (s + 1) * 8 - 1. `block_bits`: bits of a block's last word beyond cell 128 - 1 are ignored.
All inputs are finite; a program needn't handle non-finite values.
Results may differ from the reference program's by a relative error of at most 0.0002.
Values sent between devices are 32-bit elements; how exact they have to be, the bound alone decides.
A program may use at most 64 MiB of HBM per device.

```python
import math
import jax
import jax.numpy as jnp
from jax import lax

CZ = 8
NX = 64
NY = 128
STEPS = 4
NODES = 12
PAST = 10
LEVELS = 2
NZ = 128
OCC = 128
ALL_OCC = 2048
WORDS = 5


def draw_block_ids(key, part):
    key = jax.random.fold_in(key, 11)
    slabs = NZ // CZ
    keys = jax.random.split(key, slabs)

    def one_slab(slab_key, slab):
        chosen = jax.random.permutation(slab_key, CZ * NX)[:OCC]
        return chosen.astype(jnp.int32) + slab * (CZ * NX)
    picked = jax.vmap(one_slab)(keys, jnp.arange(slabs, dtype=jnp.int32))
    return picked.reshape(slabs * OCC).astype(jnp.int32)


def touch_ends(array, key, smallest, top_value):
    longest = array.shape.index(max(array.shape))
    spots = []
    for shift in (0, 1):
        where = [jax.random.randint(jax.random.fold_in(key, axis), (), 0, length) for axis, length in enumerate(array.shape)]
        where[longest] = (where[longest] + shift) % array.shape[longest]
        spots.append(tuple(where))
    return array.at[spots[0]].set(smallest).at[spots[1]].set(top_value)


def shard_levels(rng, dims, cuts, low, high):
    def one(dim, blocks):
        draws = jax.random.uniform(jax.random.fold_in(jax.random.fold_in(rng, 6), dim), (blocks,), jnp.float32, low / len(cuts), high / len(cuts))
        return jnp.repeat(jnp.exp(draws), dims[dim] // blocks).reshape((-1,) + (1,) * (len(dims) - dim - 1))

    factor_of = one(*cuts[0])
    for cut in cuts[1:]:
        factor_of = factor_of * one(*cut)
    return factor_of


def centred(rng, shape, scale, bound, cuts=(), kind=jnp.bfloat16):
    level = shard_levels(rng, shape, cuts, -0.22, 0.18) if cuts else 1.0
    entries = jax.random.normal(rng, shape, jnp.float32) * scale * level
    return jnp.minimum(jnp.maximum(entries, -bound), bound).astype(kind)


def setup_inputs(seed: int = 0) -> dict:
    arg_keys = jax.random.split(jax.random.key(seed), 7)
    return {
        "start": centred(arg_keys[0], (NZ, NX, NY), 1.0, 6.0, ((0, 16),), jnp.float32),
        "source": centred(arg_keys[1], (NZ, NX, NY), 1.0, 6.0, ((0, 16),), jnp.float32),
        "past_rates": centred(arg_keys[2], (LEVELS, PAST, NZ, NX, NY), 1.0, 6.0, ((0, 2), (2, 16)), jnp.float32),
        "block_ids": draw_block_ids(jax.random.fold_in(arg_keys[6], 71), 0),
        "block_bits": touch_ends(jax.random.randint(arg_keys[4], (ALL_OCC, WORDS), 0, 2 ** 30), jax.random.fold_in(arg_keys[4], 1), 0, (2 ** 30) - 1).astype(jnp.int32),
        "block_drag": jnp.clip(jnp.exp(math.log(4.0) - 2.0794415 * jax.random.uniform(arg_keys[5], (ALL_OCC,), jnp.float32) ** shard_levels(arg_keys[5], (ALL_OCC,), ((0, 16),), -0.2, 0.2)), 0.5, 4.0),
    }


VISCOSITY = 0.25
STEP_SIZE = 0.02


def stencil_weights(count):
    points = [float(item - (count - 2)) for item in range(count)]
    result = []
    for index in range(count):
        coeffs = [1.0]
        denom = 1.0
        for other_index in range(count):
            if other_index != index:
                other = points[other_index]
                shifted = [0.0] + coeffs
                scaled = [-other * value for value in coeffs] + [0.0]
                coeffs = [first + second for first, second in zip(shifted, scaled)]
                denom = denom * (points[index] - other)
        integral = 0.0
        for power in range(len(coeffs)):
            integral = integral + coeffs[power] / (power + 1)
        result.append(integral / denom * STEP_SIZE)
    return result


def second_diff(padded):
    inner = padded[2:-2]
    total = 16.0 * (padded[1:-3] + padded[3:-1]) - (padded[:-4] + padded[4:]) - 30.0 * inner
    for axis in (1, 2):
        total = total + 16.0 * (jnp.roll(inner, 1, axis) + jnp.roll(inner, -1, axis)) - (jnp.roll(inner, 2, axis) + jnp.roll(inner, -2, axis)) - 30.0 * inner
    return total / 12.0


def quadrature(weights, stacked):
    return jnp.tensordot(weights, stacked, axes=1, precision=lax.Precision.HIGHEST)


def reference(start, source, past_rates, block_ids, block_bits, block_drag):
    weights = jnp.asarray(stencil_weights(NODES), jnp.float32)
    cells = jnp.arange(NY)
    words = jnp.take(block_bits, cells // 30, axis=1)
    coef = (jnp.right_shift(words, cells % 30) & 1).astype(jnp.float32) * block_drag[:, None]
    penalty = jnp.zeros((NZ * NX, NY), jnp.float32).at[block_ids].set(coef).reshape(NZ, NX, NY)

    def rate_of(field):
        padded = jnp.pad(field, ((2, 2), (0, 0), (0, 0)))
        return VISCOSITY * second_diff(padded) - penalty * field + source

    below = None
    rate_list = []
    defect_list = []
    for level in range(LEVELS):
        own = [past_rates[level, index] for index in range(PAST)]
        state = start
        before = start
        for node in range(STEPS + 1):
            own.append(rate_of(state))
            if node < STEPS:
                nxt = state + STEP_SIZE * own[PAST + node]
                if level > 0:
                    lower = jnp.stack(below[PAST + node + 2 - NODES:PAST + node + 2])
                    nxt = nxt + (quadrature(weights, lower) - STEP_SIZE * below[PAST + node])
                before = state
                state = nxt
        own_sum = quadrature(weights, jnp.stack(own[PAST + STEPS + 1 - NODES:PAST + STEPS + 1]))
        defect_list.append((state - before - own_sum) / STEP_SIZE)
        rate_list.append((state - start) / (STEPS * STEP_SIZE))
        below = own
    return jnp.stack(rate_list), jnp.stack(defect_list)
```

```python
import functools

import jax
import jax.numpy as jnp
from jax import lax
from jax.experimental import pallas as pl
from jax.experimental.pallas import tpu as pltpu
from jax.sharding import PartitionSpec as P

STEPS = 4
NODES = 12
PAST = 10


VISCOSITY = 0.25
STEP_SIZE = 0.02


def with_halo(x, sides, width):
    for axis, dim in sides:
        size, length = (lax.axis_size(axis), x.shape[dim])
        up = [(i, (i + 1) % size) for i in range(size - 1)]
        down = [(j, i) for i, j in up]
        last = lax.slice_in_dim(x, length - width, length, axis=dim)
        first = lax.slice_in_dim(x, 0, width, axis=dim)
        before = lax.ppermute(last, axis, up)
        after = lax.ppermute(first, axis, down)
        x = jnp.concatenate([before, x, after], axis=dim)
    return x


def from_behind(x, axis, by):
    length = lax.axis_size(axis)
    pairs = [(i, i + by) for i in range(length) if 0 <= i + by < length]
    return lax.ppermute(x, axis, pairs)


def stencil_weights(count):
    points = [float(item - (count - 2)) for item in range(count)]
    result = []
    for index in range(count):
        coeffs = [1.0]
        denom = 1.0
        for other_index in range(count):
            if other_index != index:
                other = points[other_index]
                shifted = [0.0] + coeffs
                scaled = [-other * value for value in coeffs] + [0.0]
                coeffs = [first + second for first, second in zip(shifted, scaled)]
                denom = denom * (points[index] - other)
        integral = 0.0
        for power in range(len(coeffs)):
            integral = integral + coeffs[power] / (power + 1)
        result.append(integral / denom * STEP_SIZE)
    return result


def second_diff(padded):
    inner = padded[2:-2]
    total = 16.0 * (padded[1:-3] + padded[3:-1]) - (padded[:-4] + padded[4:]) - 30.0 * inner
    for axis in (1, 2):
        total = (
            total
            + 16.0 * (jnp.roll(inner, 1, axis) + jnp.roll(inner, -1, axis))
            - (jnp.roll(inner, 2, axis) + jnp.roll(inner, -2, axis))
            - 30.0 * inner
        )
    return total / 12.0


def quadrature(weights, stacked):
    return jnp.tensordot(weights, stacked, axes=1, precision=lax.Precision.HIGHEST)


def body(start, source, past_rates, block_ids, block_bits, block_drag):
    depth, rows, cols = start.shape
    weights = jnp.asarray(stencil_weights(NODES), jnp.float32)
    cells = jnp.arange(cols)
    words = jnp.take(block_bits, cells // 30, axis=1)
    coef = (jnp.right_shift(words, cells % 30) & 1).astype(jnp.float32) * block_drag[:, None]
    local_ids = block_ids - lax.axis_index("space") * (depth * rows)
    penalty = (
        jnp.zeros((depth * rows, cols), jnp.float32)
        .at[local_ids]
        .set(coef)
        .reshape(depth, rows, cols)
    )

    def rate_of(field):
        padded = with_halo(field, (("space", 0),), 2)
        return VISCOSITY * second_diff(padded) - penalty * field + source

    level = lax.axis_index("level")
    ticks = STEPS + lax.axis_size("level")
    history = past_rates[0]
    own_init = jnp.concatenate([history, jnp.zeros((STEPS + 2, depth, rows, cols), jnp.float32)])

    def record(own, node, rate):
        inside = (node >= 0) & (node <= STEPS)
        slot = jnp.where(inside, PAST + node, PAST + STEPS + 1)
        return lax.dynamic_update_index_in_dim(own, rate, slot, 0)

    def advance(state, before, node, rate, correction):
        moving = (node >= 0) & (node < STEPS)
        nxt = state + STEP_SIZE * rate + correction
        return (jnp.where(moving, nxt, state), jnp.where(moving, state, before))

    lower_hist = from_behind(history, "level", 1)
    below_init = jnp.concatenate(
        [lower_hist, jnp.zeros((STEPS + 3, depth, rows, cols), jnp.float32)]
    )

    def tick_recv(tick, carry):
        state, before, own, below = carry
        node = tick - level
        here = jnp.clip(node, 0, STEPS)
        rate = rate_of(state)
        own = record(own, node, rate)
        lower = from_behind(rate, "level", 1)
        upper = node + 1
        slot = jnp.where((upper >= 0) & (upper <= STEPS), PAST + upper, PAST + STEPS + 2)
        below = lax.dynamic_update_index_in_dim(below, lower, slot, 0)
        stencil = lax.dynamic_slice_in_dim(below, PAST + here + 2 - NODES, NODES, 0)
        correction = quadrature(weights, stencil) - STEP_SIZE * lax.dynamic_index_in_dim(
            below, PAST + here, 0, keepdims=False
        )
        state, before = advance(state, before, node, rate, correction)
        return (state, before, own, below)

    state, before, own, below = lax.fori_loop(
        0, ticks, tick_recv, (start, start, own_init, below_init)
    )
    own_sum = quadrature(weights, own[PAST + STEPS + 1 - NODES : PAST + STEPS + 1])
    defect = (state - before - own_sum) / STEP_SIZE
    mean_rate = (state - start) / (STEPS * STEP_SIZE)
    return (mean_rate[None], defect[None])


def kernel(
    n,
    weights,
    start_ref,
    source_ref,
    past_ref,
    ids_ref,
    bits_ref,
    drag_ref,
    mean_ref,
    defect_ref,
    u_buf,
    g_buf,
    rates,
    past,
    sums,
    source,
    drag,
    acc,
    moved,
    result,
    ids,
    bits,
    scale,
    halo_send,
    halo_recv,
    move_send,
    move_recv,
    load_sem,
    out_sem,
):
    w = weights
    h = STEP_SIZE
    depth, rows, cols = source.shape
    level = lax.axis_index("level")
    s = lax.axis_index("space")
    lower, upper = jnp.maximum(s - 1, 0), jnp.minimum(s + 1, n - 1)
    has_lower, has_upper = s > 0, s < n - 1
    fields = (u_buf, g_buf)

    loads = [
        pltpu.make_async_copy(past_ref.at[0], past, load_sem.at[0]),
        pltpu.make_async_copy(start_ref, u_buf.at[0, pl.ds(2, depth)], load_sem.at[1]),
        pltpu.make_async_copy(source_ref, source, load_sem.at[2]),
        pltpu.make_async_copy(ids_ref, ids, load_sem.at[3]),
        pltpu.make_async_copy(bits_ref, bits, load_sem.at[4]),
        pltpu.make_async_copy(drag_ref, scale, load_sem.at[5]),
    ]
    for load in loads:
        load.start()

    barrier = pltpu.get_barrier_semaphore()

    def greet(where):
        pl.semaphore_signal(
            barrier, inc=1, device_id=where, device_id_type=pl.DeviceIdType.MESH
        )

    greet({"level": 1 - level})

    @pl.when(has_lower)
    def _():
        greet({"space": lower})

    @pl.when(has_upper)
    def _():
        greet({"space": upper})

    zero = jnp.zeros((2, rows, cols), jnp.float32)

    @pl.when(s == 0)
    def _():
        for field in fields:
            for q in range(field.shape[0]):
                field[q, 0:2] = zero

    @pl.when(s == n - 1)
    def _():
        for field in fields:
            for q in range(field.shape[0]):
                field[q, depth + 2 : depth + 4] = zero

    peers = 1 + has_lower.astype(jnp.int32) + has_upper.astype(jnp.int32)
    pl.semaphore_wait(barrier, peers)

    def halo(f, q):
        buf = fields[f]
        down = pltpu.make_async_remote_copy(
            src_ref=buf.at[q, pl.ds(2, 2)],
            dst_ref=buf.at[q, pl.ds(depth + 2, 2)],
            send_sem=halo_send.at[f, q, 0],
            recv_sem=halo_recv.at[f, q, 0],
            device_id={"space": lower},
            device_id_type=pl.DeviceIdType.MESH,
        )
        up = pltpu.make_async_remote_copy(
            src_ref=buf.at[q, pl.ds(depth, 2)],
            dst_ref=buf.at[q, pl.ds(0, 2)],
            send_sem=halo_send.at[f, q, 1],
            recv_sem=halo_recv.at[f, q, 1],
            device_id={"space": upper},
            device_id_type=pl.DeviceIdType.MESH,
        )
        return down, up

    def send(f, q):
        down, up = halo(f, q)
        pl.when(has_lower)(down.start)
        pl.when(has_upper)(up.start)

    def recv(f, q):
        down, up = halo(f, q)
        pl.when(has_upper)(down.wait_recv)
        pl.when(has_lower)(up.wait_recv)

    def drain(f, q):
        down, up = halo(f, q)
        pl.when(has_lower)(down.wait_send)
        pl.when(has_upper)(up.wait_send)

    def edge(step):
        @pl.loop(0, 4)
        def _(i):
            step(i + (i // 2) * (depth - 4))

    def inner(step):
        @pl.loop(2, depth - 2)
        def _(z):
            step(z)

    def every(step):
        @pl.loop(0, depth)
        def _(z):
            step(z)

    near_scale = VISCOSITY * 16.0 / 12.0
    far_scale = VISCOSITY / 12.0

    def turn(x, by, axis):
        return pltpu.roll(x, by % x.shape[axis], axis)

    def applied(buf, q, z):
        x = buf[q, z + 2]
        near = buf[q, z + 1] + buf[q, z + 3]
        far = buf[q, z] + buf[q, z + 4]
        for axis in (0, 1):
            near = near + (turn(x, 1, axis) + turn(x, -1, axis))
            far = far + (turn(x, 2, axis) + turn(x, -2, axis))
        return near_scale * near - far_scale * far - drag[z] * x

    def past_sum(z, shift):
        total = w[0] * past[shift, z]
        for i in range(shift + 1, PAST):
            total = total + w[i - shift] * past[i, z]
        return total

    def make_drag():
        for load in loads[3:]:
            load.wait()
        words = bits[...]
        cell = lax.broadcasted_iota(jnp.int32, (cols, words.shape[1]), 0)
        word = jnp.broadcast_to(words[0:1], cell.shape)
        low = jnp.zeros_like(cell)
        for i in range(1, words.shape[0]):
            word = jnp.where(cell >= 30 * i, words[i : i + 1], word)
            low = jnp.where(cell >= 30 * i, 30 * i, low)
        mask = jnp.right_shift(word, cell - low) & 1
        value = mask.astype(jnp.float32) * scale[...]
        parts = []
        for _ in range(3):
            part = value.astype(jnp.bfloat16)
            parts.append(part)
            value = value - part.astype(jnp.float32)
        local = ids[...] - s * (depth * rows)
        row = lax.broadcasted_iota(jnp.int32, (rows, local.shape[1]), 0)

        def place(z):
            pick = jnp.where(row + z * rows == local, 1.0, 0.0).astype(jnp.bfloat16)
            total = 90.0 * VISCOSITY / 12.0
            for part in reversed(parts):
                total = total + lax.dot_general(
                    pick,
                    part,
                    (((1,), (1,)), ((), ())),
                    preferred_element_type=jnp.float32,
                )
            drag[z] = total

        every(place)

    chunks = depth // 2

    def move(i, c):
        return pltpu.make_async_remote_copy(
            src_ref=moved.at[i, pl.ds(2 * c, 2)],
            dst_ref=moved.at[i, pl.ds(2 * c, 2)],
            send_sem=move_send.at[i, c],
            recv_sem=move_recv.at[i, c],
            device_id={"level": 1 - level},
            device_id_type=pl.DeviceIdType.MESH,
        )

    def store(i, c):
        target = (mean_ref, defect_ref)[i]
        return pltpu.make_async_copy(
            result.at[i, pl.ds(2 * c, 2)], target.at[0, pl.ds(2 * c, 2)], out_sem.at[i, c]
        )

    order = [0, chunks - 1] + list(range(1, chunks - 1))

    def step_u(q, z):
        rate = applied(u_buf, q, z) + source[z]
        if q < STEPS:
            u_buf[q + 1, z + 2] = u_buf[q, z + 2] + h * rate
        return rate

    @pl.when(level == 0)
    def _():
        def first(z):
            g_buf[0, z + 2] = past_sum(z, 0)

        loads[0].wait()
        edge(first)
        send(1, 0)
        loads[1].wait()
        send(0, 0)
        inner(first)

        def later(z):
            for i in range(3):
                sums[i, z] = past_sum(z, i + 1)

        every(later)
        make_drag()
        loads[2].wait()

        def step_v(q, z):
            a = applied(g_buf, q, z)
            if q == 3:
                moved[1, z] = (acc[1, z] - w[11] * a) * (1.0 / h)
                return
            extra = sums[q, z]
            v = g_buf[q, z + 2] + (h * a + extra)
            g_buf[q + 1, z + 2] = v
            if q == 0:
                acc[1, z] = -w[8] * a
            if q == 1:
                acc[1, z] = acc[1, z] - w[9] * a
            if q == 2:
                acc[1, z] = acc[1, z] + (extra + (h - w[10]) * a)
                moved[0, z] = v * (1.0 / (STEPS * h))

        def step_own(q, z):
            rate = step_u(q, z)
            if q == 0:
                rates[0, z] = rate
                acc[0, z] = -sums[2, z] - w[7] * rate
            elif q < 4:
                rates[0, z] = rates[0, z] + rate
                c = w[7 + q] if q < 3 else w[10] - h
                acc[0, z] = acc[0, z] - c * rate
            if q == 3:
                result[0, z] = rates[0, z] * (1.0 / STEPS)
            if q == 4:
                result[1, z] = (acc[0, z] - w[11] * rate) * (1.0 / h)

        for q in range(5):
            if q < 4:
                recv(1, q)
                edge(functools.partial(step_v, q))
                if q < 3:
                    send(1, q + 1)
                if q == 2:
                    for c in order[:2]:
                        move(0, c).start()
                if q == 3:
                    for c in order[:2]:
                        move(1, c).start()
                inner(functools.partial(step_v, q))
                if q == 2:
                    for c in order[2:]:
                        move(0, c).start()
                if q == 3:
                    for c in order[2:]:
                        move(1, c).start()
            recv(0, q)
            edge(functools.partial(step_own, q))
            if q < 4:
                send(0, q + 1)
            inner(functools.partial(step_own, q))
            if q == 3:
                for c in order:
                    store(0, c).start()
        for c in order:
            store(1, c).start()
        for i in range(2):
            for c in order:
                move(i, c).wait_send()

    @pl.when(level == 1)
    def _():
        loads[1].wait()
        send(0, 0)
        make_drag()
        loads[2].wait()
        loads[0].wait()

        def step(q, z):
            if q < 5:
                rate = step_u(q, z)
                rates[q, z] = rate
            if q == 0:
                acc[1, z] = -past_sum(z, 3) - w[7] * rate
            if q == 1:
                g_buf[0, z + 2] = u_buf[0, z + 2] + (w[10] * rates[0, z] + w[11] * rate)
            if q >= 2:
                f = applied(g_buf, q - 2, z) + source[z]
                if q == 5:
                    acc[1, z] = (acc[1, z] - w[11] * f) * (1.0 / h)
                    return
                gain = h * (f - rates[q - 1, z]) + w[11] * rate
                for m in range(q):
                    gain = gain + w[m + 11 - q] * rates[m, z]
                b = g_buf[q - 2, z + 2] + gain
                g_buf[q - 1, z + 2] = b
                less = -w[6 + q] * f
                if q == 4:
                    less = less + gain
                    acc[0, z] = (b - u_buf[0, z + 2]) * (1.0 / (STEPS * h))
                acc[1, z] = acc[1, z] + less

        for q in range(6):
            if q < 5:
                recv(0, q)
            if q >= 2:
                recv(1, q - 2)
            edge(functools.partial(step, q))
            if q < 4:
                send(0, q + 1)
            if 1 <= q < 5:
                send(1, q - 1)
            inner(functools.partial(step, q))

        for i in range(2):
            for c in order:
                move(i, c).wait_recv()
                for z in (2 * c, 2 * c + 1):
                    result[i, z] = acc[i, z] + moved[i, z]
                store(i, c).start()

    for q in range(5):
        drain(0, q)
    for q in range(4):
        drain(1, q)
    for i in range(2):
        for c in order:
            store(i, c).wait()


def fused(n, start, source, past_rates, block_ids, block_bits, block_drag):
    shape = start.shape
    depth, rows, cols = shape
    padded = (depth + 4, rows, cols)
    occupied = block_ids.shape[0]
    words = block_bits.shape[1]
    f32 = jnp.float32
    anywhere = pl.BlockSpec(memory_space=pl.ANY)
    weights = tuple(stencil_weights(NODES))
    out = jax.ShapeDtypeStruct((1,) + shape, f32)
    chunks = depth // 2
    return pl.pallas_call(
        functools.partial(kernel, n, weights),
        out_shape=(out, out),
        in_specs=[anywhere] * 6,
        out_specs=(anywhere, anywhere),
        scratch_shapes=[
            pltpu.VMEM((5,) + padded, f32),
            pltpu.VMEM((4,) + padded, f32),
            pltpu.VMEM((5,) + shape, f32),
            pltpu.VMEM((PAST,) + shape, f32),
            pltpu.VMEM((3,) + shape, f32),
            pltpu.VMEM(shape, f32),
            pltpu.VMEM(shape, f32),
            pltpu.VMEM((2,) + shape, f32),
            pltpu.VMEM((2,) + shape, f32),
            pltpu.VMEM((2,) + shape, f32),
            pltpu.VMEM((1, occupied), jnp.int32),
            pltpu.VMEM((words, occupied), jnp.int32),
            pltpu.VMEM((1, occupied), f32),
            pltpu.SemaphoreType.DMA((2, 5, 2)),
            pltpu.SemaphoreType.DMA((2, 5, 2)),
            pltpu.SemaphoreType.DMA((2, chunks)),
            pltpu.SemaphoreType.DMA((2, chunks)),
            pltpu.SemaphoreType.DMA((6,)),
            pltpu.SemaphoreType.DMA((2, chunks)),
        ],
        compiler_params=pltpu.CompilerParams(
            collective_id=0, has_side_effects=True, vmem_limit_bytes=60 * 2**20
        ),
    )(
        start,
        source,
        past_rates,
        block_ids.reshape(1, occupied),
        block_bits.T,
        block_drag.reshape(1, occupied),
    )


def solution(mesh):
    in_specs = (
        P("space", None, None),
        P("space", None, None),
        P("level", None, "space", None, None),
        P("space"),
        P("space", None),
        P("space"),
    )
    out_specs = (P("level", "space", None, None), P("level", "space", None, None))
    part = body
    if mesh.shape["level"] == 2:
        part = functools.partial(fused, mesh.shape["space"])
    return jax.shard_map(part, mesh=mesh, in_specs=in_specs, out_specs=out_specs, check_vma=False)
```

```python
import functools

import jax
import jax.numpy as jnp
from jax import lax
from jax.experimental import pallas as pl
from jax.experimental.pallas import tpu as pltpu
from jax.sharding import PartitionSpec as P

STEPS = 4
NODES = 12
PAST = 10


VISCOSITY = 0.25
STEP_SIZE = 0.02


def with_halo(x, sides, width):
    for axis, dim in sides:
        size, length = (lax.axis_size(axis), x.shape[dim])
        up = [(i, (i + 1) % size) for i in range(size - 1)]
        down = [(j, i) for i, j in up]
        last = lax.slice_in_dim(x, length - width, length, axis=dim)
        first = lax.slice_in_dim(x, 0, width, axis=dim)
        before = lax.ppermute(last, axis, up)
        after = lax.ppermute(first, axis, down)
        x = jnp.concatenate([before, x, after], axis=dim)
    return x


def from_behind(x, axis, by):
    length = lax.axis_size(axis)
    pairs = [(i, i + by) for i in range(length) if 0 <= i + by < length]
    return lax.ppermute(x, axis, pairs)


def stencil_weights(count):
    points = [float(item - (count - 2)) for item in range(count)]
    result = []
    for index in range(count):
        coeffs = [1.0]
        denom = 1.0
        for other_index in range(count):
            if other_index != index:
                other = points[other_index]
                shifted = [0.0] + coeffs
                scaled = [-other * value for value in coeffs] + [0.0]
                coeffs = [first + second for first, second in zip(shifted, scaled)]
                denom = denom * (points[index] - other)
        integral = 0.0
        for power in range(len(coeffs)):
            integral = integral + coeffs[power] / (power + 1)
        result.append(integral / denom * STEP_SIZE)
    return result


def second_diff(padded):
    inner = padded[2:-2]
    total = 16.0 * (padded[1:-3] + padded[3:-1]) - (padded[:-4] + padded[4:]) - 30.0 * inner
    for axis in (1, 2):
        total = (
            total
            + 16.0 * (jnp.roll(inner, 1, axis) + jnp.roll(inner, -1, axis))
            - (jnp.roll(inner, 2, axis) + jnp.roll(inner, -2, axis))
            - 30.0 * inner
        )
    return total / 12.0


def quadrature(weights, stacked):
    return jnp.tensordot(weights, stacked, axes=1, precision=lax.Precision.HIGHEST)


def body(start, source, past_rates, block_ids, block_bits, block_drag):
    depth, rows, cols = start.shape
    weights = jnp.asarray(stencil_weights(NODES), jnp.float32)
    cells = jnp.arange(cols)
    words = jnp.take(block_bits, cells // 30, axis=1)
    coef = (jnp.right_shift(words, cells % 30) & 1).astype(jnp.float32) * block_drag[:, None]
    local_ids = block_ids - lax.axis_index("space") * (depth * rows)
    penalty = (
        jnp.zeros((depth * rows, cols), jnp.float32)
        .at[local_ids]
        .set(coef)
        .reshape(depth, rows, cols)
    )

    def rate_of(field):
        padded = with_halo(field, (("space", 0),), 2)
        return VISCOSITY * second_diff(padded) - penalty * field + source

    level = lax.axis_index("level")
    ticks = STEPS + lax.axis_size("level")
    history = past_rates[0]
    own_init = jnp.concatenate([history, jnp.zeros((STEPS + 2, depth, rows, cols), jnp.float32)])

    def record(own, node, rate):
        inside = (node >= 0) & (node <= STEPS)
        slot = jnp.where(inside, PAST + node, PAST + STEPS + 1)
        return lax.dynamic_update_index_in_dim(own, rate, slot, 0)

    def advance(state, before, node, rate, correction):
        moving = (node >= 0) & (node < STEPS)
        nxt = state + STEP_SIZE * rate + correction
        return (jnp.where(moving, nxt, state), jnp.where(moving, state, before))

    lower_hist = from_behind(history, "level", 1)
    below_init = jnp.concatenate(
        [lower_hist, jnp.zeros((STEPS + 3, depth, rows, cols), jnp.float32)]
    )

    def tick_recv(tick, carry):
        state, before, own, below = carry
        node = tick - level
        here = jnp.clip(node, 0, STEPS)
        rate = rate_of(state)
        own = record(own, node, rate)
        lower = from_behind(rate, "level", 1)
        upper = node + 1
        slot = jnp.where((upper >= 0) & (upper <= STEPS), PAST + upper, PAST + STEPS + 2)
        below = lax.dynamic_update_index_in_dim(below, lower, slot, 0)
        stencil = lax.dynamic_slice_in_dim(below, PAST + here + 2 - NODES, NODES, 0)
        correction = quadrature(weights, stencil) - STEP_SIZE * lax.dynamic_index_in_dim(
            below, PAST + here, 0, keepdims=False
        )
        state, before = advance(state, before, node, rate, correction)
        return (state, before, own, below)

    state, before, own, below = lax.fori_loop(
        0, ticks, tick_recv, (start, start, own_init, below_init)
    )
    own_sum = quadrature(weights, own[PAST + STEPS + 1 - NODES : PAST + STEPS + 1])
    defect = (state - before - own_sum) / STEP_SIZE
    mean_rate = (state - start) / (STEPS * STEP_SIZE)
    return (mean_rate[None], defect[None])


SCHEDULE = (
    ("v", 0),
    ("s", 0),
    ("v", 1),
    ("z", 0),
    ("v", 2),
    ("z", 1),
    ("v", 3),
    ("z", 2),
    ("z", 3),
    ("z", 4),
)


def rate_series(w):
    h = STEP_SIZE

    def add(*terms):
        size = max(len(series) for _, series in terms)
        return [sum(c * series[i] for c, series in terms if i < len(series)) for i in range(size)]

    results = []
    below = None
    for level in range(2):
        state = [0.0]
        own = []
        for node in range(STEPS + 1):
            own.append(add((1.0, [1.0]), (1.0, [0.0] + state)) if node else [1.0])
            if node < STEPS:
                before = state
                state = add((1.0, state), (h, own[node]))
                if level > 0:
                    state = add(
                        (1.0, state),
                        (-h, below[node]),
                        *((w[PAST - node + m], below[m]) for m in range(node + 2)),
                    )
        last = PAST + STEPS + 1 - NODES
        defect = add(
            (1.0, state),
            (-1.0, before),
            *((-w[PAST + m - last], own[m]) for m in range(STEPS + 1)),
        )
        results.append((state, defect))
        below = own
    return results


def kernel(
    n,
    weights,
    start_ref,
    source_ref,
    past_ref,
    ids_ref,
    bits_ref,
    drag_ref,
    out_ref,
    u_buf,
    g_buf,
    past,
    sums,
    source,
    drag,
    acc,
    moved,
    result,
    share,
    ids,
    bits,
    scale,
    halo_send,
    halo_recv,
    move_send,
    move_recv,
    load_sem,
    out_sem,
):
    w = weights
    lower_coeffs, upper_coeffs = rate_series(w)
    h = STEP_SIZE
    depth, rows, cols = source.shape
    level = lax.axis_index("level")
    s = lax.axis_index("space")
    lower, upper = jnp.maximum(s - 1, 0), jnp.minimum(s + 1, n - 1)
    has_lower, has_upper = s > 0, s < n - 1
    fields = (u_buf, g_buf)

    loads = [
        pltpu.make_async_copy(past_ref.at[0], past, load_sem.at[0]),
        pltpu.make_async_copy(start_ref, u_buf.at[0, pl.ds(2, depth)], load_sem.at[1]),
        pltpu.make_async_copy(source_ref, source, load_sem.at[2]),
        pltpu.make_async_copy(ids_ref, ids, load_sem.at[3]),
        pltpu.make_async_copy(bits_ref, bits, load_sem.at[4]),
        pltpu.make_async_copy(drag_ref, scale, load_sem.at[5]),
    ]
    for load in loads:
        load.start()

    barrier = pltpu.get_barrier_semaphore()

    def greet(where):
        pl.semaphore_signal(
            barrier, inc=1, device_id=where, device_id_type=pl.DeviceIdType.MESH
        )

    greet({"level": 1 - level})

    @pl.when(has_lower)
    def _():
        greet({"space": lower})

    @pl.when(has_upper)
    def _():
        greet({"space": upper})

    zero = jnp.zeros((2, rows, cols), jnp.float32)

    @pl.when(s == 0)
    def _():
        for field in fields:
            for q in range(field.shape[0]):
                field[q, 0:2] = zero

    @pl.when(s == n - 1)
    def _():
        for field in fields:
            for q in range(field.shape[0]):
                field[q, depth + 2 : depth + 4] = zero

    def halo(f, q):
        buf = fields[f]
        down = pltpu.make_async_remote_copy(
            src_ref=buf.at[q, pl.ds(2, 2)],
            dst_ref=buf.at[q, pl.ds(depth + 2, 2)],
            send_sem=halo_send.at[f, q, 0],
            recv_sem=halo_recv.at[f, q, 0],
            device_id={"space": lower},
            device_id_type=pl.DeviceIdType.MESH,
        )
        up = pltpu.make_async_remote_copy(
            src_ref=buf.at[q, pl.ds(depth, 2)],
            dst_ref=buf.at[q, pl.ds(0, 2)],
            send_sem=halo_send.at[f, q, 1],
            recv_sem=halo_recv.at[f, q, 1],
            device_id={"space": upper},
            device_id_type=pl.DeviceIdType.MESH,
        )
        return down, up

    def send(f, q):
        down, up = halo(f, q)
        pl.when(has_lower)(down.start)
        pl.when(has_upper)(up.start)

    def recv(f, q):
        down, up = halo(f, q)
        pl.when(has_upper)(down.wait_recv)
        pl.when(has_lower)(up.wait_recv)

    def drain(f, q):
        down, up = halo(f, q)
        pl.when(has_lower)(down.wait_send)
        pl.when(has_upper)(up.wait_send)

    def edge(step):
        @pl.loop(0, 4)
        def _(i):
            step(i + (i // 2) * (depth - 4))

    def inner(step):
        @pl.loop(2, depth - 2)
        def _(z):
            step(z)

    def every(step):
        @pl.loop(0, depth)
        def _(z):
            step(z)

    near_scale = VISCOSITY * 16.0 / 12.0
    far_scale = VISCOSITY / 12.0

    def turn(x, by, axis):
        return pltpu.roll(x, by % x.shape[axis], axis)

    def applied(buf, q, z):
        x = buf[q, z + 2]
        near = buf[q, z + 1] + buf[q, z + 3]
        far = buf[q, z] + buf[q, z + 4]
        for axis in (0, 1):
            near = near + (turn(x, 1, axis) + turn(x, -1, axis))
            far = far + (turn(x, 2, axis) + turn(x, -2, axis))
        return near_scale * near - far_scale * far - drag[z] * x

    def past_sum(z, shift):
        total = w[0] * past[shift, z]
        for i in range(shift + 1, PAST):
            total = total + w[i - shift] * past[i, z]
        return total

    def make_drag():
        for load in loads[3:]:
            load.wait()
        words = bits[...]
        cell = lax.broadcasted_iota(jnp.int32, (cols, words.shape[1]), 0)
        word = jnp.broadcast_to(words[0:1], cell.shape)
        low = jnp.zeros_like(cell)
        for i in range(1, words.shape[0]):
            word = jnp.where(cell >= 30 * i, words[i : i + 1], word)
            low = jnp.where(cell >= 30 * i, 30 * i, low)
        mask = jnp.right_shift(word, cell - low) & 1
        value = mask.astype(jnp.float32) * scale[...]
        parts = []
        for _ in range(3):
            part = value.astype(jnp.bfloat16)
            parts.append(part)
            value = value - part.astype(jnp.float32)
        local = ids[...] - s * (depth * rows)
        row = lax.broadcasted_iota(jnp.int32, (rows, local.shape[1]), 0)

        def place(z):
            pick = jnp.where(row + z * rows == local, 1.0, 0.0).astype(jnp.bfloat16)
            total = 90.0 * VISCOSITY / 12.0
            for part in reversed(parts):
                total = total + lax.dot_general(
                    pick,
                    part,
                    (((1,), (1,)), ((), ())),
                    preferred_element_type=jnp.float32,
                )
            drag[z] = total

        every(place)

    chunks = depth // 2

    def move(i, c):
        return pltpu.make_async_remote_copy(
            src_ref=moved.at[i, pl.ds(2 * c, 2)],
            dst_ref=moved.at[i, pl.ds(2 * c, 2)],
            send_sem=move_send.at[i, c],
            recv_sem=move_recv.at[i, c],
            device_id={"level": 1 - level},
            device_id_type=pl.DeviceIdType.MESH,
        )

    def store(i, c, origin=None):
        part = pl.ds(2 * c, 2)
        return pltpu.make_async_copy((result if origin is None else origin).at[i, part], out_ref.at[i, part], out_sem.at[i, c])

    order = [0, chunks - 1] + list(range(1, chunks - 1))

    def first(z):
        g_buf[0, z + 2] = past_sum(z, 0)

    def step_z(coeffs, q, z):
        rate = applied(u_buf, q, z)
        if q == 0:
            rate = rate + source[z]
            acc[0, z] = coeffs[0][0] * rate
            acc[1, z] = coeffs[1][0] * rate - (past_sum(z, 3) if coeffs is upper_coeffs else sums[2, z])
        for i in range(2):
            if 0 < q < len(coeffs[i]):
                acc[i, z] = acc[i, z] + coeffs[i][q] * rate
        if q + 1 < len(coeffs[1]):
            u_buf[q + 1, z + 2] = rate

    def round_z(coeffs, q):
        recv(0, q)
        edge(functools.partial(step_z, coeffs, q))
        if q + 1 < len(coeffs[1]):
            send(0, q + 1)
        inner(functools.partial(step_z, coeffs, q))

    @pl.when(level == 0)
    def _():
        loads[0].wait()
        edge(first)

    loads[1].wait()
    peers = 1 + has_lower.astype(jnp.int32) + has_upper.astype(jnp.int32)
    pl.semaphore_wait(barrier, peers)

    @pl.when(level == 0)
    def _():
        send(1, 0)
        inner(first)

        def later(z):
            for i in range(3):
                sums[i, z] = past_sum(z, i + 1)

        every(later)
        make_drag()
        loads[2].wait()

        def step_v(q, z):
            a = applied(g_buf, q, z)
            if q == 3:
                moved[1, z] = share[z] - w[11] * a
                return
            extra = sums[q, z]
            v = g_buf[q, z + 2] + (h * a + extra)
            g_buf[q + 1, z + 2] = v
            if q == 0:
                share[z] = -w[8] * a
            if q == 1:
                share[z] = share[z] - w[9] * a
            if q == 2:
                share[z] = share[z] + (extra + (h - w[10]) * a)
                moved[0, z] = v

        def round_v(q):
            recv(1, q)
            edge(functools.partial(step_v, q))
            if q < 3:
                send(1, q + 1)
            if q >= 2:
                for c in order[:2]:
                    move(q - 2, c).start()
            inner(functools.partial(step_v, q))
            if q >= 2:
                for c in order[2:]:
                    move(q - 2, c).start()

        for task in SCHEDULE:
            kind, q = task
            if kind == "s":
                send(0, 0)
            if kind == "v":
                round_v(q)
            if kind == "z":
                round_z(lower_coeffs, q)
        for i in range(2):
            for c in order:
                store(i, c, acc).start()
        for i in range(2):
            for c in order:
                move(i, c).wait_send()

    @pl.when(level == 1)
    def _():
        send(0, 0)
        make_drag()
        loads[2].wait()
        loads[0].wait()
        for q in range(6):
            round_z(upper_coeffs, q)
        for i in range(2):
            for c in order:
                move(i, c).wait_recv()
                for z in (2 * c, 2 * c + 1):
                    result[i, z] = acc[i, z] + moved[i, z]
                store(i, c).start()

    for q in range(5):
        drain(0, q)

    @pl.when(level == 0)
    def _():
        for q in range(4):
            drain(1, q)

    @pl.when(level == 1)
    def _():
        drain(0, 5)

    for i in range(2):
        for c in order:
            store(i, c).wait()


def fused(n, start, source, past_rates, block_ids, block_bits, block_drag):
    shape = start.shape
    depth, rows, cols = shape
    padded = (depth + 4, rows, cols)
    occupied = block_ids.shape[0]
    words = block_bits.shape[1]
    f32 = jnp.float32
    anywhere = pl.BlockSpec(memory_space=pl.ANY)
    weights = tuple(stencil_weights(NODES))
    chunks = depth // 2
    both = pl.pallas_call(
        functools.partial(kernel, n, weights),
        out_shape=jax.ShapeDtypeStruct((2,) + shape, f32),
        in_specs=[anywhere] * 6,
        out_specs=anywhere,
        scratch_shapes=[
            pltpu.VMEM((6,) + padded, f32),
            pltpu.VMEM((4,) + padded, f32),
            pltpu.VMEM((PAST,) + shape, f32),
            pltpu.VMEM((3,) + shape, f32),
            pltpu.VMEM(shape, f32),
            pltpu.VMEM(shape, f32),
            pltpu.VMEM((2,) + shape, f32),
            pltpu.VMEM((2,) + shape, f32),
            pltpu.VMEM((2,) + shape, f32),
            pltpu.VMEM(shape, f32),
            pltpu.VMEM((1, occupied), jnp.int32),
            pltpu.VMEM((words, occupied), jnp.int32),
            pltpu.VMEM((1, occupied), f32),
            pltpu.SemaphoreType.DMA((2, 6, 2)),
            pltpu.SemaphoreType.DMA((2, 6, 2)),
            pltpu.SemaphoreType.DMA((2, chunks)),
            pltpu.SemaphoreType.DMA((2, chunks)),
            pltpu.SemaphoreType.DMA((6,)),
            pltpu.SemaphoreType.DMA((2, chunks)),
        ],
        compiler_params=pltpu.CompilerParams(
            collective_id=0, has_side_effects=True, vmem_limit_bytes=60 * 2**20
        ),
    )(
        start,
        source,
        past_rates,
        block_ids.reshape(1, occupied),
        block_bits.T,
        block_drag.reshape(1, occupied),
    )
    return both[:1] * (1.0 / (STEPS * STEP_SIZE)), both[1:] * (1.0 / STEP_SIZE)


def solution(mesh):
    in_specs = (
        P("space", None, None),
        P("space", None, None),
        P("level", None, "space", None, None),
        P("space"),
        P("space", None),
        P("space"),
    )
    out_specs = (P("level", "space", None, None), P("level", "space", None, None))
    part = body
    if mesh.shape["level"] == 2:
        part = functools.partial(fused, mesh.shape["space"])
    return jax.shard_map(part, mesh=mesh, in_specs=in_specs, out_specs=out_specs, check_vma=False)
```

```python
import functools

import jax
import jax.numpy as jnp
from jax import lax
from jax.experimental import pallas as pl
from jax.experimental.pallas import tpu as pltpu
from jax.sharding import PartitionSpec as P

STEPS = 4
NODES = 12
PAST = 10


VISCOSITY = 0.25
STEP_SIZE = 0.02


def with_halo(x, sides, width):
    for axis, dim in sides:
        size, length = (lax.axis_size(axis), x.shape[dim])
        up = [(i, (i + 1) % size) for i in range(size - 1)]
        down = [(j, i) for i, j in up]
        last = lax.slice_in_dim(x, length - width, length, axis=dim)
        first = lax.slice_in_dim(x, 0, width, axis=dim)
        before = lax.ppermute(last, axis, up)
        after = lax.ppermute(first, axis, down)
        x = jnp.concatenate([before, x, after], axis=dim)
    return x


def from_behind(x, axis, by):
    length = lax.axis_size(axis)
    pairs = [(i, i + by) for i in range(length) if 0 <= i + by < length]
    return lax.ppermute(x, axis, pairs)


def stencil_weights(count):
    points = [float(item - (count - 2)) for item in range(count)]
    result = []
    for index in range(count):
        coeffs = [1.0]
        denom = 1.0
        for other_index in range(count):
            if other_index != index:
                other = points[other_index]
                shifted = [0.0] + coeffs
                scaled = [-other * value for value in coeffs] + [0.0]
                coeffs = [first + second for first, second in zip(shifted, scaled)]
                denom = denom * (points[index] - other)
        integral = 0.0
        for power in range(len(coeffs)):
            integral = integral + coeffs[power] / (power + 1)
        result.append(integral / denom * STEP_SIZE)
    return result


def second_diff(padded):
    inner = padded[2:-2]
    total = 16.0 * (padded[1:-3] + padded[3:-1]) - (padded[:-4] + padded[4:]) - 30.0 * inner
    for axis in (1, 2):
        total = (
            total
            + 16.0 * (jnp.roll(inner, 1, axis) + jnp.roll(inner, -1, axis))
            - (jnp.roll(inner, 2, axis) + jnp.roll(inner, -2, axis))
            - 30.0 * inner
        )
    return total / 12.0


def quadrature(weights, stacked):
    return jnp.tensordot(weights, stacked, axes=1, precision=lax.Precision.HIGHEST)


def body(start, source, past_rates, block_ids, block_bits, block_drag):
    depth, rows, cols = start.shape
    weights = jnp.asarray(stencil_weights(NODES), jnp.float32)
    cells = jnp.arange(cols)
    words = jnp.take(block_bits, cells // 30, axis=1)
    coef = (jnp.right_shift(words, cells % 30) & 1).astype(jnp.float32) * block_drag[:, None]
    local_ids = block_ids - lax.axis_index("space") * (depth * rows)
    penalty = (
        jnp.zeros((depth * rows, cols), jnp.float32)
        .at[local_ids]
        .set(coef)
        .reshape(depth, rows, cols)
    )

    def rate_of(field):
        padded = with_halo(field, (("space", 0),), 2)
        return VISCOSITY * second_diff(padded) - penalty * field + source

    level = lax.axis_index("level")
    ticks = STEPS + lax.axis_size("level")
    history = past_rates[0]
    own_init = jnp.concatenate([history, jnp.zeros((STEPS + 2, depth, rows, cols), jnp.float32)])

    def record(own, node, rate):
        inside = (node >= 0) & (node <= STEPS)
        slot = jnp.where(inside, PAST + node, PAST + STEPS + 1)
        return lax.dynamic_update_index_in_dim(own, rate, slot, 0)

    def advance(state, before, node, rate, correction):
        moving = (node >= 0) & (node < STEPS)
        nxt = state + STEP_SIZE * rate + correction
        return (jnp.where(moving, nxt, state), jnp.where(moving, state, before))

    lower_hist = from_behind(history, "level", 1)
    below_init = jnp.concatenate(
        [lower_hist, jnp.zeros((STEPS + 3, depth, rows, cols), jnp.float32)]
    )

    def tick_recv(tick, carry):
        state, before, own, below = carry
        node = tick - level
        here = jnp.clip(node, 0, STEPS)
        rate = rate_of(state)
        own = record(own, node, rate)
        lower = from_behind(rate, "level", 1)
        upper = node + 1
        slot = jnp.where((upper >= 0) & (upper <= STEPS), PAST + upper, PAST + STEPS + 2)
        below = lax.dynamic_update_index_in_dim(below, lower, slot, 0)
        stencil = lax.dynamic_slice_in_dim(below, PAST + here + 2 - NODES, NODES, 0)
        correction = quadrature(weights, stencil) - STEP_SIZE * lax.dynamic_index_in_dim(
            below, PAST + here, 0, keepdims=False
        )
        state, before = advance(state, before, node, rate, correction)
        return (state, before, own, below)

    state, before, own, below = lax.fori_loop(
        0, ticks, tick_recv, (start, start, own_init, below_init)
    )
    own_sum = quadrature(weights, own[PAST + STEPS + 1 - NODES : PAST + STEPS + 1])
    defect = (state - before - own_sum) / STEP_SIZE
    mean_rate = (state - start) / (STEPS * STEP_SIZE)
    return (mean_rate[None], defect[None])


SCHEDULE = (
    ("s", 0),
    ("v", 0),
    ("z", 0),
    ("v", 1),
    ("z", 1),
    ("v", 2),
    ("z", 2),
    ("v", 3),
    ("z", 3),
    ("z", 4),
)


def rate_series(w):
    h = STEP_SIZE

    def add(*terms):
        size = max(len(series) for _, series in terms)
        return [sum(c * series[i] for c, series in terms if i < len(series)) for i in range(size)]

    results = []
    below = None
    for level in range(2):
        state = [0.0]
        own = []
        for node in range(STEPS + 1):
            own.append(add((1.0, [1.0]), (1.0, [0.0] + state)) if node else [1.0])
            if node < STEPS:
                before = state
                state = add((1.0, state), (h, own[node]))
                if level > 0:
                    state = add(
                        (1.0, state),
                        (-h, below[node]),
                        *((w[PAST - node + m], below[m]) for m in range(node + 2)),
                    )
        last = PAST + STEPS + 1 - NODES
        defect = add(
            (1.0, state),
            (-1.0, before),
            *((-w[PAST + m - last], own[m]) for m in range(STEPS + 1)),
        )
        results.append((state, defect))
        below = own
    return results


def kernel(
    n,
    weights,
    start_ref,
    source_ref,
    past_ref,
    ids_ref,
    bits_ref,
    drag_ref,
    out_ref,
    u_buf,
    g_buf,
    past,
    sums,
    source,
    drag,
    acc,
    moved,
    result,
    share,
    ids,
    bits,
    scale,
    halo_send,
    halo_recv,
    move_send,
    move_recv,
    load_sem,
    out_sem,
):
    w = weights
    lower_coeffs, upper_coeffs = rate_series(w)
    h = STEP_SIZE
    depth, rows, cols = source.shape
    level = lax.axis_index("level")
    s = lax.axis_index("space")
    lower, upper = jnp.maximum(s - 1, 0), jnp.minimum(s + 1, n - 1)
    has_lower, has_upper = s > 0, s < n - 1
    fields = (u_buf, g_buf)

    loads = [
        pltpu.make_async_copy(past_ref.at[0], past, load_sem.at[0]),
        pltpu.make_async_copy(start_ref, u_buf.at[0, pl.ds(2, depth)], load_sem.at[1]),
        pltpu.make_async_copy(source_ref, source, load_sem.at[2]),
        pltpu.make_async_copy(ids_ref, ids, load_sem.at[3]),
        pltpu.make_async_copy(bits_ref, bits, load_sem.at[4]),
        pltpu.make_async_copy(drag_ref, scale, load_sem.at[5]),
    ]
    for load in loads:
        load.start()

    barrier = pltpu.get_barrier_semaphore()

    def greet(where):
        pl.semaphore_signal(
            barrier, inc=1, device_id=where, device_id_type=pl.DeviceIdType.MESH
        )

    greet({"level": 1 - level})

    @pl.when(has_lower)
    def _():
        greet({"space": lower})

    @pl.when(has_upper)
    def _():
        greet({"space": upper})

    zero = jnp.zeros((2, rows, cols), jnp.float32)

    @pl.when(s == 0)
    def _():
        for field in fields:
            for q in range(field.shape[0]):
                field[q, 0:2] = zero

    @pl.when(s == n - 1)
    def _():
        for field in fields:
            for q in range(field.shape[0]):
                field[q, depth + 2 : depth + 4] = zero

    def halo(f, q):
        buf = fields[f]
        down = pltpu.make_async_remote_copy(
            src_ref=buf.at[q, pl.ds(2, 2)],
            dst_ref=buf.at[q, pl.ds(depth + 2, 2)],
            send_sem=halo_send.at[f, q, 0],
            recv_sem=halo_recv.at[f, q, 0],
            device_id={"space": lower},
            device_id_type=pl.DeviceIdType.MESH,
        )
        up = pltpu.make_async_remote_copy(
            src_ref=buf.at[q, pl.ds(depth, 2)],
            dst_ref=buf.at[q, pl.ds(0, 2)],
            send_sem=halo_send.at[f, q, 1],
            recv_sem=halo_recv.at[f, q, 1],
            device_id={"space": upper},
            device_id_type=pl.DeviceIdType.MESH,
        )
        return down, up

    def send(f, q):
        down, up = halo(f, q)
        pl.when(has_lower)(down.start)
        pl.when(has_upper)(up.start)

    def recv(f, q):
        down, up = halo(f, q)
        pl.when(has_upper)(down.wait_recv)
        pl.when(has_lower)(up.wait_recv)

    def drain(f, q):
        down, up = halo(f, q)
        pl.when(has_lower)(down.wait_send)
        pl.when(has_upper)(up.wait_send)

    def edge(step):
        @pl.loop(0, 4)
        def _(i):
            step(i + (i // 2) * (depth - 4))

    def inner(step):
        @pl.loop(2, depth - 2)
        def _(z):
            step(z)

    def every(step):
        @pl.loop(0, depth)
        def _(z):
            step(z)

    near_scale = VISCOSITY * 16.0 / 12.0
    far_scale = VISCOSITY / 12.0

    def turn(x, by, axis):
        return pltpu.roll(x, by % x.shape[axis], axis)

    def applied(buf, q, z):
        x = buf[q, z + 2]
        near = buf[q, z + 1] + buf[q, z + 3]
        far = buf[q, z] + buf[q, z + 4]
        for axis in (0, 1):
            near = near + (turn(x, 1, axis) + turn(x, -1, axis))
            far = far + (turn(x, 2, axis) + turn(x, -2, axis))
        return near_scale * near - far_scale * far - drag[z] * x

    def past_sum(z, shift):
        total = w[0] * past[shift, z]
        for i in range(shift + 1, PAST):
            total = total + w[i - shift] * past[i, z]
        return total

    def make_drag():
        for load in loads[3:]:
            load.wait()
        words = bits[...]
        cell = lax.broadcasted_iota(jnp.int32, (cols, words.shape[1]), 0)
        word = jnp.broadcast_to(words[0:1], cell.shape)
        low = jnp.zeros_like(cell)
        for i in range(1, words.shape[0]):
            word = jnp.where(cell >= 30 * i, words[i : i + 1], word)
            low = jnp.where(cell >= 30 * i, 30 * i, low)
        mask = jnp.right_shift(word, cell - low) & 1
        value = mask.astype(jnp.float32) * scale[...]
        parts = []
        for _ in range(3):
            part = value.astype(jnp.bfloat16)
            parts.append(part)
            value = value - part.astype(jnp.float32)
        local = ids[...] - s * (depth * rows)
        row = lax.broadcasted_iota(jnp.int32, (rows, local.shape[1]), 0)

        def place(z):
            pick = jnp.where(row + z * rows == local, 1.0, 0.0).astype(jnp.bfloat16)
            total = 90.0 * VISCOSITY / 12.0
            for part in reversed(parts):
                total = total + lax.dot_general(
                    pick,
                    part,
                    (((1,), (1,)), ((), ())),
                    preferred_element_type=jnp.float32,
                )
            drag[z] = total

        every(place)

    chunks = depth // 2

    def move(i, c):
        return pltpu.make_async_remote_copy(
            src_ref=moved.at[i, pl.ds(2 * c, 2)],
            dst_ref=moved.at[i, pl.ds(2 * c, 2)],
            send_sem=move_send.at[i, c],
            recv_sem=move_recv.at[i, c],
            device_id={"level": 1 - level},
            device_id_type=pl.DeviceIdType.MESH,
        )

    def store(i, c, origin=None):
        part = pl.ds(2 * c, 2)
        return pltpu.make_async_copy((result if origin is None else origin).at[i, part], out_ref.at[i, part], out_sem.at[i, c])

    order = [0, chunks - 1] + list(range(1, chunks - 1))

    def first(z):
        g_buf[0, z + 2] = past_sum(z, 0)

    def step_z(coeffs, q, z):
        rate = applied(u_buf, q, z)
        if q == 0:
            rate = rate + source[z]
            acc[0, z] = coeffs[0][0] * rate
            acc[1, z] = coeffs[1][0] * rate - (past_sum(z, 3) if coeffs is upper_coeffs else sums[2, z])
        for i in range(2):
            if 0 < q < len(coeffs[i]):
                acc[i, z] = acc[i, z] + coeffs[i][q] * rate
        if q + 1 < len(coeffs[1]):
            u_buf[q + 1, z + 2] = rate

    def round_z(coeffs, q):
        recv(0, q)
        edge(functools.partial(step_z, coeffs, q))
        if q + 1 < len(coeffs[1]):
            send(0, q + 1)
        inner(functools.partial(step_z, coeffs, q))

    @pl.when(level == 0)
    def _():
        loads[0].wait()
        edge(first)

    loads[1].wait()
    peers = 1 + has_lower.astype(jnp.int32) + has_upper.astype(jnp.int32)
    pl.semaphore_wait(barrier, peers)

    @pl.when(level == 0)
    def _():
        send(1, 0)
        inner(first)

        def later(z):
            for i in range(3):
                sums[i, z] = past_sum(z, i + 1)

        every(later)
        make_drag()
        loads[2].wait()

        def step_v(q, z):
            a = applied(g_buf, q, z)
            if q == 3:
                moved[1, z] = share[z] - w[11] * a
                return
            extra = sums[q, z]
            v = g_buf[q, z + 2] + (h * a + extra)
            g_buf[q + 1, z + 2] = v
            if q == 0:
                share[z] = -w[8] * a
            if q == 1:
                share[z] = share[z] - w[9] * a
            if q == 2:
                share[z] = share[z] + (extra + (h - w[10]) * a)
                moved[0, z] = v

        def round_v(q):
            recv(1, q)
            edge(functools.partial(step_v, q))
            if q < 3:
                send(1, q + 1)
            if q >= 2:
                for c in order[:2]:
                    move(q - 2, c).start()
            inner(functools.partial(step_v, q))
            if q >= 2:
                for c in order[2:]:
                    move(q - 2, c).start()

        for task in SCHEDULE:
            kind, q = task
            if kind == "s":
                send(0, 0)
            if kind == "v":
                round_v(q)
            if kind == "z":
                round_z(lower_coeffs, q)
        for i in range(2):
            for c in order:
                store(i, c, acc).start()
        for i in range(2):
            for c in order:
                move(i, c).wait_send()

    @pl.when(level == 1)
    def _():
        send(0, 0)
        make_drag()
        loads[2].wait()
        loads[0].wait()
        for q in range(6):
            round_z(upper_coeffs, q)
        for i in range(2):
            for c in order:
                move(i, c).wait_recv()
                for z in (2 * c, 2 * c + 1):
                    result[i, z] = acc[i, z] + moved[i, z]
                store(i, c).start()

    for q in range(5):
        drain(0, q)

    @pl.when(level == 0)
    def _():
        for q in range(4):
            drain(1, q)

    @pl.when(level == 1)
    def _():
        drain(0, 5)

    for i in range(2):
        for c in order:
            store(i, c).wait()


def fused(n, start, source, past_rates, block_ids, block_bits, block_drag):
    shape = start.shape
    depth, rows, cols = shape
    padded = (depth + 4, rows, cols)
    occupied = block_ids.shape[0]
    words = block_bits.shape[1]
    f32 = jnp.float32
    anywhere = pl.BlockSpec(memory_space=pl.ANY)
    weights = tuple(stencil_weights(NODES))
    chunks = depth // 2
    both = pl.pallas_call(
        functools.partial(kernel, n, weights),
        out_shape=jax.ShapeDtypeStruct((2,) + shape, f32),
        in_specs=[anywhere] * 6,
        out_specs=anywhere,
        scratch_shapes=[
            pltpu.VMEM((6,) + padded, f32),
            pltpu.VMEM((4,) + padded, f32),
            pltpu.VMEM((PAST,) + shape, f32),
            pltpu.VMEM((3,) + shape, f32),
            pltpu.VMEM(shape, f32),
            pltpu.VMEM(shape, f32),
            pltpu.VMEM((2,) + shape, f32),
            pltpu.VMEM((2,) + shape, f32),
            pltpu.VMEM((2,) + shape, f32),
            pltpu.VMEM(shape, f32),
            pltpu.VMEM((1, occupied), jnp.int32),
            pltpu.VMEM((words, occupied), jnp.int32),
            pltpu.VMEM((1, occupied), f32),
            pltpu.SemaphoreType.DMA((2, 6, 2)),
            pltpu.SemaphoreType.DMA((2, 6, 2)),
            pltpu.SemaphoreType.DMA((2, chunks)),
            pltpu.SemaphoreType.DMA((2, chunks)),
            pltpu.SemaphoreType.DMA((6,)),
            pltpu.SemaphoreType.DMA((2, chunks)),
        ],
        compiler_params=pltpu.CompilerParams(
            collective_id=0, has_side_effects=True, vmem_limit_bytes=60 * 2**20
        ),
    )(
        start,
        source,
        past_rates,
        block_ids.reshape(1, occupied),
        block_bits.T,
        block_drag.reshape(1, occupied),
    )
    return both[:1] * (1.0 / (STEPS * STEP_SIZE)), both[1:] * (1.0 / STEP_SIZE)


def solution(mesh):
    in_specs = (
        P("space", None, None),
        P("space", None, None),
        P("level", None, "space", None, None),
        P("space"),
        P("space", None),
        P("space"),
    )
    out_specs = (P("level", "space", None, None), P("level", "space", None, None))
    part = body
    if mesh.shape["level"] == 2:
        part = functools.partial(fused, mesh.shape["space"])
    return jax.shard_map(part, mesh=mesh, in_specs=in_specs, out_specs=out_specs, check_vma=False)
```

```python
import functools

import jax
import jax.numpy as jnp
from jax import lax
from jax.experimental import pallas as pl
from jax.experimental.pallas import tpu as pltpu
from jax.sharding import PartitionSpec as P

STEPS = 4
NODES = 12
PAST = 10


VISCOSITY = 0.25
STEP_SIZE = 0.02


def with_halo(x, sides, width):
    for axis, dim in sides:
        size, length = (lax.axis_size(axis), x.shape[dim])
        up = [(i, (i + 1) % size) for i in range(size - 1)]
        down = [(j, i) for i, j in up]
        last = lax.slice_in_dim(x, length - width, length, axis=dim)
        first = lax.slice_in_dim(x, 0, width, axis=dim)
        before = lax.ppermute(last, axis, up)
        after = lax.ppermute(first, axis, down)
        x = jnp.concatenate([before, x, after], axis=dim)
    return x


def from_behind(x, axis, by):
    length = lax.axis_size(axis)
    pairs = [(i, i + by) for i in range(length) if 0 <= i + by < length]
    return lax.ppermute(x, axis, pairs)


def stencil_weights(count):
    points = [float(item - (count - 2)) for item in range(count)]
    result = []
    for index in range(count):
        coeffs = [1.0]
        denom = 1.0
        for other_index in range(count):
            if other_index != index:
                other = points[other_index]
                shifted = [0.0] + coeffs
                scaled = [-other * value for value in coeffs] + [0.0]
                coeffs = [first + second for first, second in zip(shifted, scaled)]
                denom = denom * (points[index] - other)
        integral = 0.0
        for power in range(len(coeffs)):
            integral = integral + coeffs[power] / (power + 1)
        result.append(integral / denom * STEP_SIZE)
    return result


def second_diff(padded):
    inner = padded[2:-2]
    total = 16.0 * (padded[1:-3] + padded[3:-1]) - (padded[:-4] + padded[4:]) - 30.0 * inner
    for axis in (1, 2):
        total = (
            total
            + 16.0 * (jnp.roll(inner, 1, axis) + jnp.roll(inner, -1, axis))
            - (jnp.roll(inner, 2, axis) + jnp.roll(inner, -2, axis))
            - 30.0 * inner
        )
    return total / 12.0


def quadrature(weights, stacked):
    return jnp.tensordot(weights, stacked, axes=1, precision=lax.Precision.HIGHEST)


def body(start, source, past_rates, block_ids, block_bits, block_drag):
    depth, rows, cols = start.shape
    weights = jnp.asarray(stencil_weights(NODES), jnp.float32)
    cells = jnp.arange(cols)
    words = jnp.take(block_bits, cells // 30, axis=1)
    coef = (jnp.right_shift(words, cells % 30) & 1).astype(jnp.float32) * block_drag[:, None]
    local_ids = block_ids - lax.axis_index("space") * (depth * rows)
    penalty = (
        jnp.zeros((depth * rows, cols), jnp.float32)
        .at[local_ids]
        .set(coef)
        .reshape(depth, rows, cols)
    )

    def rate_of(field):
        padded = with_halo(field, (("space", 0),), 2)
        return VISCOSITY * second_diff(padded) - penalty * field + source

    level = lax.axis_index("level")
    ticks = STEPS + lax.axis_size("level")
    history = past_rates[0]
    own_init = jnp.concatenate([history, jnp.zeros((STEPS + 2, depth, rows, cols), jnp.float32)])

    def record(own, node, rate):
        inside = (node >= 0) & (node <= STEPS)
        slot = jnp.where(inside, PAST + node, PAST + STEPS + 1)
        return lax.dynamic_update_index_in_dim(own, rate, slot, 0)

    def advance(state, before, node, rate, correction):
        moving = (node >= 0) & (node < STEPS)
        nxt = state + STEP_SIZE * rate + correction
        return (jnp.where(moving, nxt, state), jnp.where(moving, state, before))

    lower_hist = from_behind(history, "level", 1)
    below_init = jnp.concatenate(
        [lower_hist, jnp.zeros((STEPS + 3, depth, rows, cols), jnp.float32)]
    )

    def tick_recv(tick, carry):
        state, before, own, below = carry
        node = tick - level
        here = jnp.clip(node, 0, STEPS)
        rate = rate_of(state)
        own = record(own, node, rate)
        lower = from_behind(rate, "level", 1)
        upper = node + 1
        slot = jnp.where((upper >= 0) & (upper <= STEPS), PAST + upper, PAST + STEPS + 2)
        below = lax.dynamic_update_index_in_dim(below, lower, slot, 0)
        stencil = lax.dynamic_slice_in_dim(below, PAST + here + 2 - NODES, NODES, 0)
        correction = quadrature(weights, stencil) - STEP_SIZE * lax.dynamic_index_in_dim(
            below, PAST + here, 0, keepdims=False
        )
        state, before = advance(state, before, node, rate, correction)
        return (state, before, own, below)

    state, before, own, below = lax.fori_loop(
        0, ticks, tick_recv, (start, start, own_init, below_init)
    )
    own_sum = quadrature(weights, own[PAST + STEPS + 1 - NODES : PAST + STEPS + 1])
    defect = (state - before - own_sum) / STEP_SIZE
    mean_rate = (state - start) / (STEPS * STEP_SIZE)
    return (mean_rate[None], defect[None])


SCHEDULE = (
    ("s", 0),
    ("v", 0),
    ("z", 0),
    ("v", 1),
    ("z", 1),
    ("v", 2),
    ("z", 2),
    ("v", 3),
    ("z", 3),
    ("z", 4),
)


def rate_series(w):
    h = STEP_SIZE

    def add(*terms):
        size = max(len(series) for _, series in terms)
        return [sum(c * series[i] for c, series in terms if i < len(series)) for i in range(size)]

    results = []
    below = None
    for level in range(2):
        state = [0.0]
        own = []
        for node in range(STEPS + 1):
            own.append(add((1.0, [1.0]), (1.0, [0.0] + state)) if node else [1.0])
            if node < STEPS:
                before = state
                state = add((1.0, state), (h, own[node]))
                if level > 0:
                    state = add(
                        (1.0, state),
                        (-h, below[node]),
                        *((w[PAST - node + m], below[m]) for m in range(node + 2)),
                    )
        last = PAST + STEPS + 1 - NODES
        defect = add(
            (1.0, state),
            (-1.0, before),
            *((-w[PAST + m - last], own[m]) for m in range(STEPS + 1)),
        )
        results.append((state, defect))
        below = own
    return results


def kernel(
    n,
    weights,
    start_ref,
    source_ref,
    past_ref,
    ids_ref,
    bits_ref,
    drag_ref,
    out_ref,
    u_buf,
    g_buf,
    past,
    sums,
    source,
    drag,
    acc,
    moved,
    result,
    share,
    ids,
    bits,
    scale,
    halo_send,
    halo_recv,
    move_send,
    move_recv,
    load_sem,
    out_sem,
):
    w = weights
    lower_coeffs, upper_coeffs = rate_series(w)
    h = STEP_SIZE
    depth, rows, cols = source.shape
    level = lax.axis_index("level")
    s = lax.axis_index("space")
    lower, upper = jnp.maximum(s - 1, 0), jnp.minimum(s + 1, n - 1)
    has_lower, has_upper = s > 0, s < n - 1
    fields = (u_buf, g_buf)

    loads = [
        pltpu.make_async_copy(past_ref.at[0], past, load_sem.at[0]),
        pltpu.make_async_copy(start_ref, u_buf.at[0, pl.ds(2, depth)], load_sem.at[1]),
        pltpu.make_async_copy(source_ref, source, load_sem.at[2]),
        pltpu.make_async_copy(ids_ref, ids, load_sem.at[3]),
        pltpu.make_async_copy(bits_ref, bits, load_sem.at[4]),
        pltpu.make_async_copy(drag_ref, scale, load_sem.at[5]),
    ]
    for load in loads:
        load.start()

    barrier = pltpu.get_barrier_semaphore()

    def greet(where):
        pl.semaphore_signal(
            barrier, inc=1, device_id=where, device_id_type=pl.DeviceIdType.MESH
        )

    greet({"level": 1 - level})

    @pl.when(has_lower)
    def _():
        greet({"space": lower})

    @pl.when(has_upper)
    def _():
        greet({"space": upper})

    zero = jnp.zeros((2, rows, cols), jnp.float32)

    @pl.when(s == 0)
    def _():
        for field in fields:
            for q in range(field.shape[0]):
                field[q, 0:2] = zero

    @pl.when(s == n - 1)
    def _():
        for field in fields:
            for q in range(field.shape[0]):
                field[q, depth + 2 : depth + 4] = zero

    def halo(f, q):
        buf = fields[f]
        down = pltpu.make_async_remote_copy(
            src_ref=buf.at[q, pl.ds(2, 2)],
            dst_ref=buf.at[q, pl.ds(depth + 2, 2)],
            send_sem=halo_send.at[f, q, 0],
            recv_sem=halo_recv.at[f, q, 0],
            device_id={"space": lower},
            device_id_type=pl.DeviceIdType.MESH,
        )
        up = pltpu.make_async_remote_copy(
            src_ref=buf.at[q, pl.ds(depth, 2)],
            dst_ref=buf.at[q, pl.ds(0, 2)],
            send_sem=halo_send.at[f, q, 1],
            recv_sem=halo_recv.at[f, q, 1],
            device_id={"space": upper},
            device_id_type=pl.DeviceIdType.MESH,
        )
        return down, up

    def send(f, q):
        down, up = halo(f, q)
        pl.when(has_lower)(down.start)
        pl.when(has_upper)(up.start)

    def recv(f, q):
        down, up = halo(f, q)
        pl.when(has_upper)(down.wait_recv)
        pl.when(has_lower)(up.wait_recv)

    def drain(f, q):
        down, up = halo(f, q)
        pl.when(has_lower)(down.wait_send)
        pl.when(has_upper)(up.wait_send)

    def edge(step):
        @pl.loop(0, 4, unroll=2)
        def _(i):
            step(i + (i // 2) * (depth - 4))

    def inner(step):
        @pl.loop(2, depth - 2, unroll=2)
        def _(z):
            step(z)

    def every(step):
        @pl.loop(0, depth)
        def _(z):
            step(z)

    near_scale = VISCOSITY * 16.0 / 12.0
    far_scale = VISCOSITY / 12.0

    def turn(x, by, axis):
        return pltpu.roll(x, by % x.shape[axis], axis)

    def applied(buf, q, z):
        x = buf[q, z + 2]
        near = buf[q, z + 1] + buf[q, z + 3]
        far = buf[q, z] + buf[q, z + 4]
        for axis in (0, 1):
            near = near + (turn(x, 1, axis) + turn(x, -1, axis))
            far = far + (turn(x, 2, axis) + turn(x, -2, axis))
        return near_scale * near - far_scale * far - drag[z] * x

    def past_sum(z, shift):
        total = w[0] * past[shift, z]
        for i in range(shift + 1, PAST):
            total = total + w[i - shift] * past[i, z]
        return total

    def make_drag():
        for load in loads[3:]:
            load.wait()
        words = bits[...]
        cell = lax.broadcasted_iota(jnp.int32, (cols, words.shape[1]), 0)
        word = jnp.broadcast_to(words[0:1], cell.shape)
        low = jnp.zeros_like(cell)
        for i in range(1, words.shape[0]):
            word = jnp.where(cell >= 30 * i, words[i : i + 1], word)
            low = jnp.where(cell >= 30 * i, 30 * i, low)
        mask = jnp.right_shift(word, cell - low) & 1
        value = mask.astype(jnp.float32) * scale[...]
        parts = []
        for _ in range(3):
            part = value.astype(jnp.bfloat16)
            parts.append(part)
            value = value - part.astype(jnp.float32)
        local = ids[...] - s * (depth * rows)
        row = lax.broadcasted_iota(jnp.int32, (rows, local.shape[1]), 0)

        def place(z):
            pick = jnp.where(row + z * rows == local, 1.0, 0.0).astype(jnp.bfloat16)
            total = 90.0 * VISCOSITY / 12.0
            for part in reversed(parts):
                total = total + lax.dot_general(
                    pick,
                    part,
                    (((1,), (1,)), ((), ())),
                    preferred_element_type=jnp.float32,
                )
            drag[z] = total

        every(place)

    chunks = depth // 2

    def move(i, c):
        return pltpu.make_async_remote_copy(
            src_ref=moved.at[i, pl.ds(2 * c, 2)],
            dst_ref=moved.at[i, pl.ds(2 * c, 2)],
            send_sem=move_send.at[i, c],
            recv_sem=move_recv.at[i, c],
            device_id={"level": 1 - level},
            device_id_type=pl.DeviceIdType.MESH,
        )

    def store(i, c, origin=None):
        part = pl.ds(2 * c, 2)
        return pltpu.make_async_copy((result if origin is None else origin).at[i, part], out_ref.at[i, part], out_sem.at[i, c])

    order = [0, chunks - 1] + list(range(1, chunks - 1))

    def first(z):
        g_buf[0, z + 2] = past_sum(z, 0)

    def step_z(coeffs, q, z):
        rate = applied(u_buf, q, z)
        if q == 0:
            rate = rate + source[z]
            acc[0, z] = coeffs[0][0] * rate
            acc[1, z] = coeffs[1][0] * rate - (past_sum(z, 3) if coeffs is upper_coeffs else sums[2, z])
        for i in range(2):
            if 0 < q < len(coeffs[i]):
                acc[i, z] = acc[i, z] + coeffs[i][q] * rate
        if q + 1 < len(coeffs[1]):
            u_buf[q + 1, z + 2] = rate

    def round_z(coeffs, q):
        recv(0, q)
        edge(functools.partial(step_z, coeffs, q))
        if q + 1 < len(coeffs[1]):
            send(0, q + 1)
        inner(functools.partial(step_z, coeffs, q))

    @pl.when(level == 0)
    def _():
        loads[0].wait()
        edge(first)

    loads[1].wait()
    peers = 1 + has_lower.astype(jnp.int32) + has_upper.astype(jnp.int32)
    pl.semaphore_wait(barrier, peers)

    @pl.when(level == 0)
    def _():
        send(1, 0)
        inner(first)

        def later(z):
            for i in range(3):
                sums[i, z] = past_sum(z, i + 1)

        every(later)
        make_drag()
        loads[2].wait()

        def step_v(q, z):
            a = applied(g_buf, q, z)
            if q == 3:
                moved[1, z] = share[z] - w[11] * a
                return
            extra = sums[q, z]
            v = g_buf[q, z + 2] + (h * a + extra)
            g_buf[q + 1, z + 2] = v
            if q == 0:
                share[z] = -w[8] * a
            if q == 1:
                share[z] = share[z] - w[9] * a
            if q == 2:
                share[z] = share[z] + (extra + (h - w[10]) * a)
                moved[0, z] = v

        def round_v(q):
            recv(1, q)
            edge(functools.partial(step_v, q))
            if q < 3:
                send(1, q + 1)
            if q >= 2:
                for c in order[:2]:
                    move(q - 2, c).start()
            inner(functools.partial(step_v, q))
            if q >= 2:
                for c in order[2:]:
                    move(q - 2, c).start()

        for task in SCHEDULE:
            kind, q = task
            if kind == "s":
                send(0, 0)
            if kind == "v":
                round_v(q)
            if kind == "z":
                round_z(lower_coeffs, q)
        for i in range(2):
            for c in order:
                store(i, c, acc).start()
        for i in range(2):
            for c in order:
                move(i, c).wait_send()

    @pl.when(level == 1)
    def _():
        send(0, 0)
        make_drag()
        loads[2].wait()
        loads[0].wait()
        for q in range(6):
            round_z(upper_coeffs, q)
        for i in range(2):
            for c in order:
                move(i, c).wait_recv()
                for z in (2 * c, 2 * c + 1):
                    result[i, z] = acc[i, z] + moved[i, z]
                store(i, c).start()

    for q in range(5):
        drain(0, q)

    @pl.when(level == 0)
    def _():
        for q in range(4):
            drain(1, q)

    @pl.when(level == 1)
    def _():
        drain(0, 5)

    for i in range(2):
        for c in order:
            store(i, c).wait()


def fused(n, start, source, past_rates, block_ids, block_bits, block_drag):
    shape = start.shape
    depth, rows, cols = shape
    padded = (depth + 4, rows, cols)
    occupied = block_ids.shape[0]
    words = block_bits.shape[1]
    f32 = jnp.float32
    anywhere = pl.BlockSpec(memory_space=pl.ANY)
    weights = tuple(stencil_weights(NODES))
    chunks = depth // 2
    both = pl.pallas_call(
        functools.partial(kernel, n, weights),
        out_shape=jax.ShapeDtypeStruct((2,) + shape, f32),
        in_specs=[anywhere] * 6,
        out_specs=anywhere,
        scratch_shapes=[
            pltpu.VMEM((6,) + padded, f32),
            pltpu.VMEM((4,) + padded, f32),
            pltpu.VMEM((PAST,) + shape, f32),
            pltpu.VMEM((3,) + shape, f32),
            pltpu.VMEM(shape, f32),
            pltpu.VMEM(shape, f32),
            pltpu.VMEM((2,) + shape, f32),
            pltpu.VMEM((2,) + shape, f32),
            pltpu.VMEM((2,) + shape, f32),
            pltpu.VMEM(shape, f32),
            pltpu.VMEM((1, occupied), jnp.int32),
            pltpu.VMEM((words, occupied), jnp.int32),
            pltpu.VMEM((1, occupied), f32),
            pltpu.SemaphoreType.DMA((2, 6, 2)),
            pltpu.SemaphoreType.DMA((2, 6, 2)),
            pltpu.SemaphoreType.DMA((2, chunks)),
            pltpu.SemaphoreType.DMA((2, chunks)),
            pltpu.SemaphoreType.DMA((6,)),
            pltpu.SemaphoreType.DMA((2, chunks)),
        ],
        compiler_params=pltpu.CompilerParams(
            collective_id=0, has_side_effects=True, vmem_limit_bytes=60 * 2**20
        ),
    )(
        start,
        source,
        past_rates,
        block_ids.reshape(1, occupied),
        block_bits.T,
        block_drag.reshape(1, occupied),
    )
    return both[:1] * (1.0 / (STEPS * STEP_SIZE)), both[1:] * (1.0 / STEP_SIZE)


def solution(mesh):
    in_specs = (
        P("space", None, None),
        P("space", None, None),
        P("level", None, "space", None, None),
        P("space"),
        P("space", None),
        P("space"),
    )
    out_specs = (P("level", "space", None, None), P("level", "space", None, None))
    part = body
    if mesh.shape["level"] == 2:
        part = functools.partial(fused, mesh.shape["space"])
    return jax.shard_map(part, mesh=mesh, in_specs=in_specs, out_specs=out_specs, check_vma=False)
```
